32 devices in a mesh: space: 8 (over z, x), blk: 4 (over y, core).
Axes of the slice: x: 2, y: 2, z: 4, core: 2. Of those that a mesh axis runs over, the one named last changes fastest.
Arguments:
- snapshots: float32 [32, 256, 5, 2048], P('blk', 'space'), may hold values from -72 to 72
- weights: float32 [5, 2048], P(None, 'space'), may hold values from 0.05 to 31, as said below
- frequencies: int32 [16], replicated, may hold values from 0 to 127, as said below
- offsets: int32 [32], P('blk'), may hold values from 0 to 4095
- eigenvectors: float32 [16, 2, 32, 4], replicated, may hold values from -6 to 6
Outputs:
- modes: float32 [16, 2, 4, 5, 2048], P('blk', None, None, None, 'space')
- energies: float32 [16, 4], P('blk')
The draws below stay inside these ranges and needn't reach their ends.
Inputs may be any that keep to these rules, and one draw needn't show every extreme that they name: `weights`: positive. `frequencies`: distinct indices.
All inputs are finite; a program needn't handle non-finite values.
Results may differ from the reference program's by a relative error of at most 0.000073.
Values sent between devices are 32-bit elements; how exact they have to be, the bound alone decides.
A program may use at most 384 MiB of HBM per device.

```python
import math
import jax
import jax.numpy as jnp
from jax import lax

NT = 256
BLOCKS = 32
NF = 16
VARS = 5
MODES = 4
CELLS = 2048


def draw_snapshots(key, part):
    key = jax.random.fold_in(key, 11)
    key_var, key_cell, key_base = jax.random.split(key, 3)
    var_scale = jnp.exp(jax.random.uniform(key_var, (VARS, 1), jnp.float32, math.log(0.3), math.log(3.0)))
    shape = (BLOCKS, NT, VARS, CELLS)
    cell_scale = jnp.exp(jax.random.uniform(key_cell, (1, CELLS), jnp.float32, math.log(0.3), math.log(3.0)))
    base = jnp.clip(jax.random.normal(key_base, shape, jnp.float32), -6.0, 6.0)
    return (base * (var_scale * cell_scale)).astype(jnp.float32)


def draw_weights(key, part):
    key = jax.random.fold_in(key, 23)
    key_var, key_cell = jax.random.split(key, 2)
    var_gain = jnp.exp(jax.random.uniform(key_var, (VARS, 1), jnp.float32, math.log(0.2), math.log(5.0)))
    position = jnp.arange(CELLS, dtype=jnp.float32)[None, :] / CELLS
    rising = jnp.exp(math.log(3.0) * position)
    rough = jax.random.uniform(key_cell, (1, CELLS), jnp.float32, 0.5, 1.5)
    return (var_gain * rising * rough).astype(jnp.float32)


def draw_frequencies(key, part):
    key = jax.random.fold_in(key, 37)
    key_pick, key_order = jax.random.split(key, 2)
    inner = 1 + jax.random.permutation(key_pick, NT // 2 - 2)[:NF - 2]
    ends = jnp.array([0, NT // 2 - 1], dtype=jnp.int32)
    chosen = jnp.concatenate([ends, inner.astype(jnp.int32)])
    order = jax.random.permutation(key_order, NF)
    return chosen[order].astype(jnp.int32)


def plant(result, rng, smallest, high):
    longest = result.shape.index(max(result.shape))
    spots = []
    for shift in (0, 1):
        where = [jax.random.randint(jax.random.fold_in(rng, axis), (), 0, length) for axis, length in enumerate(result.shape)]
        where[longest] = (where[longest] + shift) % result.shape[longest]
        spots.append(tuple(where))
    return result.at[spots[0]].set(smallest).at[spots[1]].set(high)


def scatter_about(own_key, shape, spread, bound, kind=jnp.bfloat16):
    return jnp.clip(spread * jax.random.normal(own_key, shape, jnp.float32), -bound, bound).astype(kind)


def setup_inputs(seed: int = 0) -> dict:
    streams_of = jax.random.split(jax.random.key(seed), 6)
    snapshots = draw_snapshots(jax.random.fold_in(streams_of[5], 71), 0)
    weights = draw_weights(jax.random.fold_in(streams_of[5], 71), 0)
    frequencies = draw_frequencies(jax.random.fold_in(streams_of[5], 71), 0)
    offsets = plant(jax.random.randint(streams_of[3], (BLOCKS,), 0, NT * 16), jax.random.fold_in(streams_of[3], 1), 0, (NT * 16) - 1).astype(jnp.int32)
    eigenvectors = scatter_about(streams_of[4], (NF, 2, BLOCKS, MODES), 1.0, 6.0, jnp.float32)
    return dict(snapshots=snapshots, weights=weights, frequencies=frequencies, offsets=offsets, eigenvectors=eigenvectors)


HIGH = lax.Precision.HIGHEST

def window_twiddle(count, frequencies):
    times = jnp.arange(count, dtype=jnp.int32)
    turns = frequencies[:, None] * times[None, :] % count
    angles = 2.0 * math.pi / count * turns.astype(jnp.float32)
    phases = 2.0 * math.pi / count * times.astype(jnp.float32)
    window = 0.5 - 0.5 * jnp.cos(phases)
    window = window / jnp.sqrt(jnp.sum(window * window))
    return jnp.concatenate([window[None, :] * jnp.cos(angles), -window[None, :] * jnp.sin(angles)], axis=0)

def rotate(raw, frequencies, offsets, count):
    turns = offsets[:, None] * frequencies[None, :] % count
    angles = 2.0 * math.pi / count * turns.astype(jnp.float32)
    cosine = jnp.cos(angles)[:, :, None, None]
    sine = jnp.sin(angles)[:, :, None, None]
    real_part = raw[:, 0]
    imag_part = raw[:, 1]
    return jnp.stack([real_part * cosine + imag_part * sine, imag_part * cosine - real_part * sine], axis=1)

def quadratic(gram_real, gram_imag, eigenvectors):
    vec_real = eigenvectors[:, 0]
    vec_imag = eigenvectors[:, 1]
    prod_real = jnp.einsum('fbd,fdm->fbm', gram_real, vec_real, precision=HIGH) - jnp.einsum('fbd,fdm->fbm', gram_imag, vec_imag, precision=HIGH)
    prod_imag = jnp.einsum('fbd,fdm->fbm', gram_real, vec_imag, precision=HIGH) + jnp.einsum('fbd,fdm->fbm', gram_imag, vec_real, precision=HIGH)
    return lax.optimization_barrier(jnp.sum(vec_real * prod_real + vec_imag * prod_imag, axis=1))

def rebuild(real_part, imag_part, eigenvectors):
    vec_real = eigenvectors[:, 0]
    vec_imag = eigenvectors[:, 1]
    mode_real = jnp.einsum('bfvc,fbm->fmvc', real_part, vec_real, precision=HIGH) - jnp.einsum('bfvc,fbm->fmvc', imag_part, vec_imag, precision=HIGH)
    mode_imag = jnp.einsum('bfvc,fbm->fmvc', real_part, vec_imag, precision=HIGH) + jnp.einsum('bfvc,fbm->fmvc', imag_part, vec_real, precision=HIGH)
    return jnp.stack([mode_real, mode_imag], axis=1)

def reference(snapshots, weights, frequencies, offsets, eigenvectors):
    twiddle = window_twiddle(NT, frequencies)

    def one_block(block):
        out = jnp.einsum('pt,tvc->pvc', twiddle, block, precision=HIGH)
        return out.reshape(2, NF, VARS, CELLS)
    raw = lax.map(one_block, snapshots)
    coeffs = rotate(raw, frequencies, offsets, NT)
    total = jnp.sum(weights)
    real_part = coeffs[:, 0]
    imag_part = coeffs[:, 1]
    w_real = real_part * weights
    w_imag = imag_part * weights
    scale = 1.0 / (BLOCKS * total)
    gram_real = (jnp.einsum('bfvc,dfvc->fbd', w_real, real_part, precision=HIGH) + jnp.einsum('bfvc,dfvc->fbd', w_imag, imag_part, precision=HIGH)) * scale
    gram_imag = (jnp.einsum('bfvc,dfvc->fbd', w_real, imag_part, precision=HIGH) - jnp.einsum('bfvc,dfvc->fbd', w_imag, real_part, precision=HIGH)) * scale
    energies = quadratic(gram_real, gram_imag, eigenvectors)
    unscaled = rebuild(real_part, imag_part, eigenvectors)
    divisor = jnp.sqrt(BLOCKS * energies + 1e-06)
    modes = unscaled / divisor[:, None, :, None, None]
    return (modes, energies)
```

```python
import math

import jax
import jax.numpy as jnp
from jax import lax
from jax.sharding import PartitionSpec as P

HIGH = lax.Precision.HIGHEST


def projection(snap_shape, frequencies, offsets, eigenvectors, count, dtype=jnp.float32):
    items, times = snap_shape[0], snap_shape[1]
    num_freq = frequencies.shape[0]
    all_times = jnp.arange(count, dtype=jnp.int32)
    phases = 2.0 * math.pi / count * all_times.astype(jnp.float32)
    window = 0.5 - 0.5 * jnp.cos(phases)
    norm = jnp.sqrt(jnp.sum(window * window))
    own = lax.axis_index("space") * times + jnp.arange(times, dtype=jnp.int32)
    own_window = (0.5 - 0.5 * jnp.cos(2.0 * math.pi / count * own.astype(jnp.float32))) / norm
    shifted = (own[None, :] + offsets[:, None]) % count
    turns = frequencies[:, None, None] * shifted[None] % count
    angles = 2.0 * math.pi / count * turns.astype(jnp.float32)
    cosine = own_window * jnp.cos(angles)
    sine = -own_window * jnp.sin(angles)
    vec = lax.dynamic_slice_in_dim(eigenvectors, lax.axis_index("blk") * items, items, 2)
    vec = vec.transpose(0, 1, 3, 2)[..., None]
    vec_real, vec_imag = vec[:, 0], vec[:, 1]
    cosine, sine = cosine[:, None], sine[:, None]
    real = vec_real * cosine - vec_imag * sine
    imag = vec_real * sine + vec_imag * cosine
    return jnp.stack([real, imag], axis=1)


def local(snapshots, weights, frequencies, offsets, eigenvectors):
    num_blocks = eigenvectors.shape[2]
    count = snapshots.shape[1] * lax.axis_size("space")
    matrix = projection(snapshots.shape, frequencies, offsets, eigenvectors, count)
    partial = jnp.einsum("fpmbt,btvc->fpmvc", matrix, snapshots, precision=HIGH)
    part = lax.psum_scatter(partial, "blk", scatter_dimension=0, tiled=True)
    unscaled = lax.psum_scatter(part, "space", scatter_dimension=4, tiled=True)
    local_energy = jnp.sum(unscaled * unscaled * weights, axis=(1, 3, 4))
    energy, total = lax.psum((local_energy, jnp.sum(weights)), "space")
    energies = energy / (num_blocks * total)
    divisor = jnp.sqrt(num_blocks * energies + 1e-06)
    modes = unscaled / divisor[:, None, :, None, None]
    return (modes, energies)


def solution(mesh):
    in_specs = (P("blk", "space", None, None), P(None, "space"), P(), P("blk"), P())
    out_specs = (P("blk", None, None, None, "space"), P("blk", None))
    return jax.shard_map(local, mesh=mesh, in_specs=in_specs, out_specs=out_specs, check_vma=False)
```

```python
import functools
import math

import jax
import jax.numpy as jnp
from jax import lax
from jax.experimental import pallas as pl
from jax.experimental.pallas import tpu as pltpu
from jax.sharding import PartitionSpec as P

HIGH = lax.Precision.HIGHEST


def projection(snap_shape, frequencies, offsets, eigenvectors, count, dtype=jnp.float32):
    items, times = snap_shape[0], snap_shape[1]
    num_freq = frequencies.shape[0]
    all_times = jnp.arange(count, dtype=jnp.int32)
    phases = 2.0 * math.pi / count * all_times.astype(jnp.float32)
    window = 0.5 - 0.5 * jnp.cos(phases)
    norm = jnp.sqrt(jnp.sum(window * window))
    own = lax.axis_index("space") * times + jnp.arange(times, dtype=jnp.int32)
    own_window = (0.5 - 0.5 * jnp.cos(2.0 * math.pi / count * own.astype(jnp.float32))) / norm
    shifted = (own[None, :] + offsets[:, None]) % count
    turns = frequencies[:, None, None] * shifted[None] % count
    angles = 2.0 * math.pi / count * turns.astype(jnp.float32)
    cosine = own_window * jnp.cos(angles)
    sine = -own_window * jnp.sin(angles)
    vec = lax.dynamic_slice_in_dim(eigenvectors, lax.axis_index("blk") * items, items, 2)
    vec = vec.transpose(0, 1, 3, 2)[..., None]
    vec_real, vec_imag = vec[:, 0], vec[:, 1]
    cosine, sine = cosine[:, None], sine[:, None]
    real = vec_real * cosine - vec_imag * sine
    imag = vec_real * sine + vec_imag * cosine
    return jnp.stack([real, imag], axis=1)


def local_plain(snapshots, weights, frequencies, offsets, eigenvectors):
    num_blocks = eigenvectors.shape[2]
    count = snapshots.shape[1] * lax.axis_size("space")
    matrix = projection(snapshots.shape, frequencies, offsets, eigenvectors, count)
    partial = jnp.einsum("fpmbt,btvc->fpmvc", matrix, snapshots, precision=HIGH)
    part = lax.psum_scatter(partial, "blk", scatter_dimension=0, tiled=True)
    unscaled = lax.psum_scatter(part, "space", scatter_dimension=4, tiled=True)
    local_energy = jnp.sum(unscaled * unscaled * weights, axis=(1, 3, 4))
    energy, total = lax.psum((local_energy, jnp.sum(weights)), "space")
    energies = energy / (num_blocks * total)
    divisor = jnp.sqrt(num_blocks * energies + 1e-06)
    modes = unscaled / divisor[:, None, :, None, None]
    return (modes, energies)


MESH = pl.DeviceIdType.MESH
LANES = 128


def reduce_kernel(
    depth, x_ref, a_ref, w_ref, out_ref, e_ref,
    xbuf, acat, keep, send0, r0, r1, r2, s2, r3, acc, esend, erecv,
    x_sem, s0_sem, t0_sem, s1_sem, t1_sem, s2_sem, t2_sem, s3_sem, t3_sem, se_sem, te_sem,
):
    num_vars = w_ref.shape[0]
    width = out_ref.shape[2]
    rows = a_ref.shape[2]
    half = rows // 2
    total_rows = 4 * rows
    inner = a_ref.shape[3]
    space, blk = lax.axis_index("space"), lax.axis_index("blk")
    z, x = space // 2, space % 2
    y, c = blk // 2, blk % 2
    size = 2 * depth
    across_core = (space, y * 2 + (1 - c))
    across_x = (z * 2 + (1 - x), blk)
    across_y = (space, (1 - y) * 2 + c)

    loads = []
    for v in range(num_vars):
        load = pltpu.make_async_copy(x_ref.at[:, v], xbuf.at[v], x_sem.at[v])
        load.start()
        loads.append(load)

    barrier = pltpu.get_barrier_semaphore()
    pl.semaphore_signal(barrier, inc=1, device_id=across_core, device_id_type=MESH)
    pl.semaphore_signal(barrier, inc=1, device_id=across_y, device_id_type=MESH)
    for d in range(1, size):
        pl.semaphore_signal(
            barrier, inc=1, device_id=(lax.rem(space + d, size), blk), device_id_type=MESH
        )

    for cr in range(2):
        for yr in range(2):
            part = a_ref[(y + yr) % 2, (c + cr) % 2]
            high = part.astype(jnp.bfloat16)
            low = (part - high.astype(jnp.float32)).astype(jnp.bfloat16)
            first = (cr * 2 + yr) * rows
            acat[first : first + rows, :] = high
            acat[total_rows + first : total_rows + first + rows, :] = low

    def project(v):
        def column(k, carry):
            for xa in range(2):
                xr = (x + xa) % 2
                cols = pl.ds(pl.multiple_of(k * (2 * width) + xa * width, width), width)
                block = xbuf[v, :, :, cols].reshape(inner, width)
                high = block.astype(jnp.bfloat16)
                low = (block - high.astype(jnp.float32)).astype(jnp.bfloat16)
                both = jnp.dot(acat[...], high, preferred_element_type=jnp.float32)
                rest = jnp.dot(acat[:total_rows, :], low, preferred_element_type=jnp.float32)
                res = both[:total_rows] + (both[total_rows:] + rest)
                for cr, buf in ((0, keep), (1, send0)):
                    for yr in range(2):
                        first = (cr * 2 + yr) * rows
                        buf[v, 0, xr, yr, k] = res[first : first + half]
                        buf[v, 1, yr, xr, k] = res[first + half : first + rows]
            return carry

        lax.fori_loop(0, depth, column, 0)

    def remote(src, dst, sem_out, sem_in, target):
        return pltpu.make_async_remote_copy(
            src_ref=src, dst_ref=dst, send_sem=sem_out, recv_sem=sem_in,
            device_id=target, device_id_type=MESH,
        )

    hop0 = [
        remote(send0.at[v], r0.at[v], s0_sem.at[v], t0_sem.at[v], across_core)
        for v in range(num_vars)
    ]
    hop1 = [
        [
            remote(keep.at[v, h, 1], r1.at[v, h], s1_sem.at[v, h], t1_sem.at[v, h], to)
            for h, to in ((0, across_x), (1, across_y))
        ]
        for v in range(num_vars)
    ]
    hop2 = [
        [
            remote(r1.at[v, h, 1], r2.at[v, h], s2_sem.at[v, h], t2_sem.at[v, h], to)
            for h, to in ((0, across_y), (1, across_x))
        ]
        for v in range(num_vars)
    ]
    hop3 = []
    for v in range(num_vars):
        group = []
        for d in range(1, depth):
            k = lax.rem(z + d, depth)
            group.append(
                remote(
                    s2.at[v, k], r3.at[v, d - 1], s3_sem.at[v, d - 1], t3_sem.at[v, d - 1],
                    (k * 2 + x, blk),
                )
            )
        hop3.append(group)

    def stage0(v):
        loads[v].wait()
        project(v)
        if v == 0:
            pl.semaphore_wait(barrier, size + 1)
        hop0[v].start()

    def stage1(v):
        hop0[v].wait_recv()
        for h in range(2):
            keep[v, h, 1] = keep[v, h, 1] + r0[v, h, 1]
            hop1[v][h].start()

    def stage2(v):
        for h in range(2):
            hop1[v][h].wait_recv()
            r1[v, h, 1] = r1[v, h, 1] + (keep[v, h, 0, 1] + r0[v, h, 0, 1])
            hop2[v][h].start()

    def stage3(v):
        for h in range(2):
            hop2[v][h].wait_recv()
            s2[v, :, h] = (keep[v, h, 0, 0] + r0[v, h, 0, 0]) + (r1[v, h, 0] + r2[v, h])
        for copy in hop3[v]:
            copy.start()

    def stage4(v):
        for copy in hop3[v]:
            copy.wait_recv()
        result = s2[v, z]
        for d in range(1, depth):
            result = result + r3[v, d - 1]
        result = result.reshape(rows, width)
        out_ref[v] = result
        term = result * result * w_ref[v : v + 1, :]
        if v == 0:
            acc[...] = term
        else:
            acc[...] = acc[...] + term

    stages = (stage0, stage1, stage2, stage3, stage4)
    for step in range(num_vars + len(stages) - 1):
        for lag, stage in enumerate(stages):
            if 0 <= step - lag < num_vars:
                stage(step - lag)

    def fold(value):
        folded = value[:, :LANES]
        for k in range(1, width // LANES):
            folded = folded + value[:, k * LANES : (k + 1) * LANES]
        return folded

    esend[:rows, :] = fold(acc[...])
    weight_sum = fold(jnp.sum(w_ref[...], axis=0, keepdims=True))
    esend[rows:, :] = jnp.broadcast_to(weight_sum, (8, LANES))
    share = []
    for d in range(1, size):
        copy = remote(
            esend, erecv.at[d - 1], se_sem.at[d - 1], te_sem.at[d - 1],
            (lax.rem(space + d, size), blk),
        )
        copy.start()
        share.append(copy)
    total = esend[...]
    for d in range(1, size):
        share[d - 1].wait_recv()
        total = total + erecv[d - 1]
    e_ref[...] = total
    for v in range(num_vars):
        hop0[v].wait_send()
        for copy in hop1[v] + hop2[v] + hop3[v]:
            copy.wait_send()
    for copy in share:
        copy.wait_send()


def reduce_modes(snapshots, matrix, weights):
    items, num_vars, times, cells = snapshots.shape
    width = weights.shape[1]
    depth = cells // width // 2
    rows = matrix.shape[2]
    inner = matrix.shape[3]
    half = rows // 2
    size = 2 * depth
    f32 = jnp.float32
    dma = pltpu.SemaphoreType.DMA
    vmem = pl.BlockSpec(memory_space=pltpu.VMEM)
    return pl.pallas_call(
        functools.partial(reduce_kernel, depth),
        out_shape=(
            jax.ShapeDtypeStruct((num_vars, rows, width), f32),
            jax.ShapeDtypeStruct((rows + 8, LANES), f32),
        ),
        in_specs=[pl.BlockSpec(memory_space=pl.ANY), vmem, vmem],
        out_specs=(vmem, vmem),
        scratch_shapes=[
            pltpu.VMEM((num_vars, items, times, cells), f32),
            pltpu.VMEM((8 * rows, inner), jnp.bfloat16),
            pltpu.VMEM((num_vars, 2, 2, 2, depth, half, width), f32),
            pltpu.VMEM((num_vars, 2, 2, 2, depth, half, width), f32),
            pltpu.VMEM((num_vars, 2, 2, 2, depth, half, width), f32),
            pltpu.VMEM((num_vars, 2, 2, depth, half, width), f32),
            pltpu.VMEM((num_vars, 2, depth, half, width), f32),
            pltpu.VMEM((num_vars, depth, 2, half, width), f32),
            pltpu.VMEM((num_vars, depth - 1, 2, half, width), f32),
            pltpu.VMEM((rows, width), f32),
            pltpu.VMEM((rows + 8, LANES), f32),
            pltpu.VMEM((size - 1, rows + 8, LANES), f32),
            dma((num_vars,)),
            dma((num_vars,)),
            dma((num_vars,)),
            dma((num_vars, 2)),
            dma((num_vars, 2)),
            dma((num_vars, 2)),
            dma((num_vars, 2)),
            dma((num_vars, depth - 1)),
            dma((num_vars, depth - 1)),
            dma((size - 1,)),
            dma((size - 1,)),
        ],
        compiler_params=pltpu.CompilerParams(
            collective_id=0, has_side_effects=True, vmem_limit_bytes=56 * 2**20
        ),
    )(snapshots, matrix, weights)


def local_kernel(snapshots, weights, frequencies, offsets, eigenvectors):
    num_blocks = eigenvectors.shape[2]
    num_freq = frequencies.shape[0]
    modes_kept = eigenvectors.shape[3]
    owned = num_freq // 4
    num_vars, width = weights.shape
    count = snapshots.shape[1] * lax.axis_size("space")
    matrix = projection(snapshots.shape, frequencies, offsets, eigenvectors, count)
    matrix = matrix.reshape(2, 2, owned * 2 * modes_kept, -1)
    raw, sums = reduce_modes(snapshots.transpose(0, 2, 1, 3), matrix, weights)
    rows = matrix.shape[2]
    lane_sum = jnp.sum(sums, axis=1)
    energy = jnp.sum(lane_sum[:rows].reshape(owned, 2, modes_kept), axis=1)
    energies = energy / (num_blocks * lane_sum[rows])
    divisor = jnp.sqrt(num_blocks * energies + 1e-06)
    unscaled = raw.reshape(num_vars, owned, 2, modes_kept, width).transpose(1, 2, 3, 0, 4)
    modes = unscaled / divisor[:, None, :, None, None]
    return (modes, energies)


def fits(mesh):
    return mesh.shape["blk"] == 4 and mesh.shape["space"] == 8


def solution(mesh):
    local = local_kernel if fits(mesh) else local_plain
    in_specs = (P("blk", "space", None, None), P(None, "space"), P(), P("blk"), P())
    out_specs = (P("blk", None, None, None, "space"), P("blk", None))
    return jax.shard_map(local, mesh=mesh, in_specs=in_specs, out_specs=out_specs, check_vma=False)
```

```python
import functools
import math

import jax
import jax.numpy as jnp
from jax import lax
from jax.experimental import pallas as pl
from jax.experimental.pallas import tpu as pltpu
from jax.sharding import PartitionSpec as P

HIGH = lax.Precision.HIGHEST


def projection(snap_shape, frequencies, offsets, eigenvectors, count, dtype=jnp.float32):
    items, times = snap_shape[0], snap_shape[1]
    num_freq = frequencies.shape[0]
    all_times = jnp.arange(count, dtype=jnp.int32)
    phases = 2.0 * math.pi / count * all_times.astype(jnp.float32)
    window = 0.5 - 0.5 * jnp.cos(phases)
    norm = jnp.sqrt(jnp.sum(window * window))
    own = lax.axis_index("space") * times + jnp.arange(times, dtype=jnp.int32)
    own_window = (0.5 - 0.5 * jnp.cos(2.0 * math.pi / count * own.astype(jnp.float32))) / norm
    shifted = (own[None, :] + offsets[:, None]) % count
    turns = frequencies[:, None, None] * shifted[None] % count
    angles = 2.0 * math.pi / count * turns.astype(jnp.float32)
    cosine = own_window * jnp.cos(angles)
    sine = -own_window * jnp.sin(angles)
    vec = lax.dynamic_slice_in_dim(eigenvectors, lax.axis_index("blk") * items, items, 2)
    vec = vec.transpose(0, 1, 3, 2)[..., None]
    vec_real, vec_imag = vec[:, 0], vec[:, 1]
    cosine, sine = cosine[:, None], sine[:, None]
    real = vec_real * cosine - vec_imag * sine
    imag = vec_real * sine + vec_imag * cosine
    return jnp.stack([real, imag], axis=1)


def local_plain(snapshots, weights, frequencies, offsets, eigenvectors):
    num_blocks = eigenvectors.shape[2]
    count = snapshots.shape[1] * lax.axis_size("space")
    matrix = projection(snapshots.shape, frequencies, offsets, eigenvectors, count)
    partial = jnp.einsum("fpmbt,btvc->fpmvc", matrix, snapshots, precision=HIGH)
    part = lax.psum_scatter(partial, "blk", scatter_dimension=0, tiled=True)
    unscaled = lax.psum_scatter(part, "space", scatter_dimension=4, tiled=True)
    local_energy = jnp.sum(unscaled * unscaled * weights, axis=(1, 3, 4))
    energy, total = lax.psum((local_energy, jnp.sum(weights)), "space")
    energies = energy / (num_blocks * total)
    divisor = jnp.sqrt(num_blocks * energies + 1e-06)
    modes = unscaled / divisor[:, None, :, None, None]
    return (modes, energies)


MESH = pl.DeviceIdType.MESH
LANES = 128


def projection_rows(freq_ref, off_ref, vec, times, parts, space, blk):
    num_freq, items = freq_ref.shape[0], off_ref.shape[0]
    modes_kept, num_blocks = vec.shape[2], vec.shape[3]
    count, inner = times * parts, items * times
    lane = lax.broadcasted_iota(jnp.int32, (1, inner), 1)
    block = lane // times
    own = lane % times + space * times
    shift = jnp.zeros_like(lane)
    for b in range(items):
        shift = jnp.where(block == b, off_ref[b], shift)
    row = lax.broadcasted_iota(jnp.int32, (num_freq, inner), 0)
    index = jnp.zeros_like(row)
    for f in range(num_freq):
        index = jnp.where(row == f, freq_ref[f], index)
    turns = (index * ((own + shift) & (count - 1))) & (count - 1)
    angles = 2.0 * math.pi / count * turns.astype(jnp.float32)
    norm = math.sqrt(sum((0.5 - 0.5 * math.cos(2.0 * math.pi * t / count)) ** 2 for t in range(count)))
    phases = 2.0 * math.pi / count * own.astype(jnp.float32)
    window = (0.5 - 0.5 * jnp.cos(phases)) * (1.0 / norm)
    full = (num_freq, 2 * modes_kept, inner)
    cosine = jnp.broadcast_to((window * jnp.cos(angles))[:, None, :], full)
    sine = jnp.broadcast_to((-window * jnp.sin(angles))[:, None, :], full)
    pick = lax.broadcasted_iota(jnp.int32, (num_blocks, inner), 0) == block + blk * items
    pick = jnp.where(pick, 1.0, 0.0)
    turned = jnp.concatenate([-vec[:, 1:2], vec[:, 0:1]], axis=1)
    flat = (num_freq * 2 * modes_kept, num_blocks)
    straight = jnp.dot(vec.reshape(flat), pick, precision=HIGH, preferred_element_type=jnp.float32)
    turned = jnp.dot(turned.reshape(flat), pick, precision=HIGH, preferred_element_type=jnp.float32)
    flat = (num_freq * 2 * modes_kept, inner)
    return straight * cosine.reshape(flat) + turned * sine.reshape(flat)


def reduce_kernel(
    depth, num_blocks, x_ref, w_hbm, vec_hbm, freq_hbm, off_hbm, out_ref, energy_ref,
    xbuf, w_ref, vec_ref, freq_ref, off_ref, raw, acat, keep, send0, r0, r1, r2, s2, r3, acc, esend, erecv,
    in_sem, x_sem, s0_sem, t0_sem, s1_sem, t1_sem, s2_sem, t2_sem, s3_sem, t3_sem, se_sem, te_sem,
):
    num_vars = w_ref.shape[0]
    width = w_ref.shape[1]
    num_freq, modes_kept = vec_ref.shape[0], vec_ref.shape[2]
    total_rows = num_freq * 2 * modes_kept
    rows = total_rows // 4
    half = rows // 2
    inner = xbuf.shape[1] * xbuf.shape[2]
    space, blk = lax.axis_index("space"), lax.axis_index("blk")
    z, x = space // 2, space % 2
    y, c = blk // 2, blk % 2
    size = 2 * depth
    across_core = (space, y * 2 + (1 - c))
    across_x = (z * 2 + (1 - x), blk)
    across_y = (space, (1 - y) * 2 + c)

    small = []
    for k, (src, dst) in enumerate(
        ((freq_hbm, freq_ref), (off_hbm, off_ref), (vec_hbm, vec_ref), (w_hbm, w_ref))
    ):
        copy = pltpu.make_async_copy(src, dst, in_sem.at[k])
        copy.start()
        small.append(copy)
    loads = []
    for v in range(num_vars):
        load = pltpu.make_async_copy(x_ref.at[:, v], xbuf.at[v], x_sem.at[v])
        load.start()
        loads.append(load)

    barrier = pltpu.get_barrier_semaphore()
    pl.semaphore_signal(barrier, inc=1, device_id=across_core, device_id_type=MESH)
    pl.semaphore_signal(barrier, inc=1, device_id=across_y, device_id_type=MESH)
    for d in range(1, size):
        pl.semaphore_signal(
            barrier, inc=1, device_id=(lax.rem(space + d, size), blk), device_id_type=MESH
        )

    for copy in small:
        copy.wait()
    matrix = projection_rows(
        freq_ref, off_ref, vec_ref[...], xbuf.shape[2], 2 * depth, space, blk
    )
    high = matrix.astype(jnp.bfloat16)
    low = (matrix - high.astype(jnp.float32)).astype(jnp.bfloat16)
    for ya in range(2):
        for ca in range(2):
            first = (ya * 2 + ca) * rows
            acat[0, (ca + c) % 2, (ya + y) % 2] = high[first : first + rows]
            acat[1, (ca + c) % 2, (ya + y) % 2] = low[first : first + rows]

    def project(v):
        def column(k, carry):
            for xa in range(2):
                xr = (x + xa) % 2
                cols = pl.ds(pl.multiple_of(k * (2 * width) + xa * width, width), width)
                block = xbuf[v, :, :, cols].reshape(inner, width)
                high = block.astype(jnp.bfloat16)
                low = (block - high.astype(jnp.float32)).astype(jnp.bfloat16)
                both = jnp.dot(acat[...].reshape(2 * total_rows, inner), high, preferred_element_type=jnp.float32)
                rest = jnp.dot(acat[0].reshape(total_rows, inner), low, preferred_element_type=jnp.float32)
                res = both[:total_rows] + (both[total_rows:] + rest)
                for cr, buf in ((0, keep), (1, send0)):
                    for yr in range(2):
                        first = (cr * 2 + yr) * rows
                        buf[v, 0, xr, yr, k] = res[first : first + half]
                        buf[v, 1, yr, xr, k] = res[first + half : first + rows]
            return carry

        lax.fori_loop(0, depth, column, 0)

    def remote(src, dst, sem_out, sem_in, target):
        return pltpu.make_async_remote_copy(
            src_ref=src, dst_ref=dst, send_sem=sem_out, recv_sem=sem_in,
            device_id=target, device_id_type=MESH,
        )

    hop0 = [
        remote(send0.at[v], r0.at[v], s0_sem.at[v], t0_sem.at[v], across_core)
        for v in range(num_vars)
    ]
    hop1 = [
        [
            remote(keep.at[v, h, 1], r1.at[v, h], s1_sem.at[v, h], t1_sem.at[v, h], to)
            for h, to in ((0, across_x), (1, across_y))
        ]
        for v in range(num_vars)
    ]
    hop2 = [
        [
            remote(r1.at[v, h, 1], r2.at[v, h], s2_sem.at[v, h], t2_sem.at[v, h], to)
            for h, to in ((0, across_y), (1, across_x))
        ]
        for v in range(num_vars)
    ]
    hop3 = []
    for v in range(num_vars):
        group = []
        for d in range(1, depth):
            k = lax.rem(z + d, depth)
            group.append(
                remote(
                    s2.at[v, k], r3.at[v, d - 1], s3_sem.at[v, d - 1], t3_sem.at[v, d - 1],
                    (k * 2 + x, blk),
                )
            )
        hop3.append(group)

    def stage0(v):
        loads[v].wait()
        project(v)
        if v == 0:
            pl.semaphore_wait(barrier, size + 1)
        hop0[v].start()

    def stage1(v):
        hop0[v].wait_recv()
        for h in range(2):
            keep[v, h, 1] = keep[v, h, 1] + r0[v, h, 1]
            hop1[v][h].start()

    def stage2(v):
        for h in range(2):
            hop1[v][h].wait_recv()
            r1[v, h, 1] = r1[v, h, 1] + (keep[v, h, 0, 1] + r0[v, h, 0, 1])
            hop2[v][h].start()

    def stage3(v):
        for h in range(2):
            hop2[v][h].wait_recv()
            s2[v, :, h] = (keep[v, h, 0, 0] + r0[v, h, 0, 0]) + (r1[v, h, 0] + r2[v, h])
        for copy in hop3[v]:
            copy.start()

    def stage4(v):
        for copy in hop3[v]:
            copy.wait_recv()
        result = s2[v, z]
        for d in range(1, depth):
            result = result + r3[v, d - 1]
        result = result.reshape(rows, width)
        raw[v] = result
        term = result * result * w_ref[v : v + 1, :]
        if v == 0:
            acc[...] = term
        else:
            acc[...] = acc[...] + term

    stages = (stage0, stage1, stage2, stage3, stage4)
    for step in range(num_vars + len(stages) - 1):
        for lag, stage in enumerate(stages):
            if 0 <= step - lag < num_vars:
                stage(step - lag)

    def fold(value):
        folded = value[:, :LANES]
        for k in range(1, width // LANES):
            folded = folded + value[:, k * LANES : (k + 1) * LANES]
        return folded

    esend[:rows, :] = fold(acc[...])
    weight_sum = fold(jnp.sum(w_ref[...], axis=0, keepdims=True))
    esend[rows:, :] = jnp.broadcast_to(weight_sum, (8, LANES))
    share = []
    for d in range(1, size):
        copy = remote(
            esend, erecv.at[d - 1], se_sem.at[d - 1], te_sem.at[d - 1],
            (lax.rem(space + d, size), blk),
        )
        copy.start()
        share.append(copy)
    total = esend[...]
    for d in range(1, size):
        share[d - 1].wait_recv()
        total = total + erecv[d - 1]
    owned = rows // (2 * modes_kept)
    pair = total[:rows].reshape(owned, 2 * modes_kept, LANES)
    pair = pair + jnp.concatenate([pair[:, modes_kept:], pair[:, :modes_kept]], axis=1)
    weight_total = jnp.sum(total[rows : rows + 1], axis=1, keepdims=True)
    energy = jnp.sum(pair, axis=2, keepdims=True) / (num_blocks * weight_total)[None]
    inverse = 1.0 / jnp.sqrt(num_blocks * energy + 1e-06)
    for v in range(num_vars):
        scaled = raw[v].reshape(owned, 2 * modes_kept, width) * inverse
        out_ref[:, 0, v] = scaled[:, :modes_kept]
        out_ref[:, 1, v] = scaled[:, modes_kept:]
    square = (modes_kept, modes_kept)
    same = lax.broadcasted_iota(jnp.int32, square, 0) == lax.broadcasted_iota(jnp.int32, square, 1)
    spread = jnp.broadcast_to(energy[:, :modes_kept], (owned, modes_kept, modes_kept))
    energy_ref[...] = jnp.sum(jnp.where(same[None], spread, 0.0), axis=1)
    for v in range(num_vars):
        hop0[v].wait_send()
        for copy in hop1[v] + hop2[v] + hop3[v]:
            copy.wait_send()
    for copy in share:
        copy.wait_send()


def reduce_modes(snapshots, weights, vectors, frequencies, offsets):
    items, num_vars, times, cells = snapshots.shape
    num_freq, _, modes_kept, num_blocks = vectors.shape
    width = weights.shape[1]
    depth = cells // width // 2
    owned = num_freq // 4
    rows = owned * 2 * modes_kept
    inner = items * times
    half = rows // 2
    size = 2 * depth
    f32 = jnp.float32
    dma = pltpu.SemaphoreType.DMA
    anywhere = pl.BlockSpec(memory_space=pl.ANY)
    vmem = pl.BlockSpec(memory_space=pltpu.VMEM)
    return pl.pallas_call(
        functools.partial(reduce_kernel, depth, num_blocks),
        out_shape=(
            jax.ShapeDtypeStruct((owned, 2, num_vars, modes_kept, width), f32),
            jax.ShapeDtypeStruct((owned, modes_kept), f32),
        ),
        in_specs=[anywhere] * 5,
        out_specs=(vmem, vmem),
        scratch_shapes=[
            pltpu.VMEM((num_vars, items, times, cells), f32),
            pltpu.VMEM((num_vars, width), f32),
            pltpu.VMEM(vectors.shape, f32),
            pltpu.SMEM(frequencies.shape, jnp.int32),
            pltpu.SMEM(offsets.shape, jnp.int32),
            pltpu.VMEM((num_vars, rows, width), f32),
            pltpu.VMEM((2, 2, 2, rows, inner), jnp.bfloat16),
            pltpu.VMEM((num_vars, 2, 2, 2, depth, half, width), f32),
            pltpu.VMEM((num_vars, 2, 2, 2, depth, half, width), f32),
            pltpu.VMEM((num_vars, 2, 2, 2, depth, half, width), f32),
            pltpu.VMEM((num_vars, 2, 2, depth, half, width), f32),
            pltpu.VMEM((num_vars, 2, depth, half, width), f32),
            pltpu.VMEM((num_vars, depth, 2, half, width), f32),
            pltpu.VMEM((num_vars, depth - 1, 2, half, width), f32),
            pltpu.VMEM((rows, width), f32),
            pltpu.VMEM((rows + 8, LANES), f32),
            pltpu.VMEM((size - 1, rows + 8, LANES), f32),
            dma((4,)),
            dma((num_vars,)),
            dma((num_vars,)),
            dma((num_vars,)),
            dma((num_vars, 2)),
            dma((num_vars, 2)),
            dma((num_vars, 2)),
            dma((num_vars, 2)),
            dma((num_vars, depth - 1)),
            dma((num_vars, depth - 1)),
            dma((size - 1,)),
            dma((size - 1,)),
        ],
        compiler_params=pltpu.CompilerParams(
            collective_id=0, has_side_effects=True, vmem_limit_bytes=56 * 2**20
        ),
    )(snapshots, weights, vectors, frequencies, offsets)


def local_kernel(snapshots, weights, frequencies, offsets, eigenvectors):
    modes, energies = reduce_modes(
        snapshots.transpose(0, 2, 1, 3), weights, eigenvectors.transpose(0, 1, 3, 2),
        frequencies, offsets,
    )
    return (modes.transpose(0, 1, 3, 2, 4), energies)


def fits(mesh):
    return mesh.shape["blk"] == 4 and mesh.shape["space"] == 8


def solution(mesh):
    local = local_kernel if fits(mesh) else local_plain
    in_specs = (P("blk", "space", None, None), P(None, "space"), P(), P("blk"), P())
    out_specs = (P("blk", None, None, None, "space"), P("blk", None))
    return jax.shard_map(local, mesh=mesh, in_specs=in_specs, out_specs=out_specs, check_vma=False)
```

```python
import functools
import math

import jax
import jax.numpy as jnp
from jax import lax
from jax.experimental import pallas as pl
from jax.experimental.pallas import tpu as pltpu
from jax.sharding import PartitionSpec as P

HIGH = lax.Precision.HIGHEST


def projection(snap_shape, frequencies, offsets, eigenvectors, count, dtype=jnp.float32):
    items, times = snap_shape[0], snap_shape[1]
    num_freq = frequencies.shape[0]
    all_times = jnp.arange(count, dtype=jnp.int32)
    phases = 2.0 * math.pi / count * all_times.astype(jnp.float32)
    window = 0.5 - 0.5 * jnp.cos(phases)
    norm = jnp.sqrt(jnp.sum(window * window))
    own = lax.axis_index("space") * times + jnp.arange(times, dtype=jnp.int32)
    own_window = (0.5 - 0.5 * jnp.cos(2.0 * math.pi / count * own.astype(jnp.float32))) / norm
    shifted = (own[None, :] + offsets[:, None]) % count
    turns = frequencies[:, None, None] * shifted[None] % count
    angles = 2.0 * math.pi / count * turns.astype(jnp.float32)
    cosine = own_window * jnp.cos(angles)
    sine = -own_window * jnp.sin(angles)
    vec = lax.dynamic_slice_in_dim(eigenvectors, lax.axis_index("blk") * items, items, 2)
    vec = vec.transpose(0, 1, 3, 2)[..., None]
    vec_real, vec_imag = vec[:, 0], vec[:, 1]
    cosine, sine = cosine[:, None], sine[:, None]
    real = vec_real * cosine - vec_imag * sine
    imag = vec_real * sine + vec_imag * cosine
    return jnp.stack([real, imag], axis=1)


def local_plain(snapshots, weights, frequencies, offsets, eigenvectors):
    num_blocks = eigenvectors.shape[2]
    count = snapshots.shape[1] * lax.axis_size("space")
    matrix = projection(snapshots.shape, frequencies, offsets, eigenvectors, count)
    partial = jnp.einsum("fpmbt,btvc->fpmvc", matrix, snapshots, precision=HIGH)
    part = lax.psum_scatter(partial, "blk", scatter_dimension=0, tiled=True)
    unscaled = lax.psum_scatter(part, "space", scatter_dimension=4, tiled=True)
    local_energy = jnp.sum(unscaled * unscaled * weights, axis=(1, 3, 4))
    energy, total = lax.psum((local_energy, jnp.sum(weights)), "space")
    energies = energy / (num_blocks * total)
    divisor = jnp.sqrt(num_blocks * energies + 1e-06)
    modes = unscaled / divisor[:, None, :, None, None]
    return (modes, energies)


MESH = pl.DeviceIdType.MESH
LANES = 128


def projection_rows(freq_ref, off_ref, vec, times, parts, space, blk):
    num_freq, items = freq_ref.shape[0], off_ref.shape[0]
    modes_kept, num_blocks = vec.shape[2], vec.shape[3]
    count, inner = times * parts, items * times
    lane = lax.broadcasted_iota(jnp.int32, (1, inner), 1)
    block = lane // times
    own = lane % times + space * times
    shift = jnp.zeros_like(lane)
    for b in range(items):
        shift = jnp.where(block == b, off_ref[b], shift)
    row = lax.broadcasted_iota(jnp.int32, (num_freq, inner), 0)
    index = jnp.zeros_like(row)
    for f in range(num_freq):
        index = jnp.where(row == f, freq_ref[f], index)
    turns = (index * ((own + shift) & (count - 1))) & (count - 1)
    angles = 2.0 * math.pi / count * turns.astype(jnp.float32)
    norm = math.sqrt(sum((0.5 - 0.5 * math.cos(2.0 * math.pi * t / count)) ** 2 for t in range(count)))
    phases = 2.0 * math.pi / count * own.astype(jnp.float32)
    window = (0.5 - 0.5 * jnp.cos(phases)) * (1.0 / norm)
    full = (num_freq, 2 * modes_kept, inner)
    cosine = jnp.broadcast_to((window * jnp.cos(angles))[:, None, :], full)
    sine = jnp.broadcast_to((-window * jnp.sin(angles))[:, None, :], full)
    pick = lax.broadcasted_iota(jnp.int32, (num_blocks, inner), 0) == block + blk * items
    pick = jnp.where(pick, 1.0, 0.0)
    turned = jnp.concatenate([-vec[:, 1:2], vec[:, 0:1]], axis=1)
    flat = (num_freq * 2 * modes_kept, num_blocks)
    straight = jnp.dot(vec.reshape(flat), pick, precision=HIGH, preferred_element_type=jnp.float32)
    turned = jnp.dot(turned.reshape(flat), pick, precision=HIGH, preferred_element_type=jnp.float32)
    flat = (num_freq * 2 * modes_kept, inner)
    return straight * cosine.reshape(flat) + turned * sine.reshape(flat)


def reduce_kernel(
    depth, num_blocks, x_ref, w_hbm, vec_hbm, freq_hbm, off_hbm, out_ref, energy_ref,
    xbuf, w_ref, vec_ref, freq_ref, off_ref, raw, acat, keep, send0, r0, r1, r2, s2, r3, acc, esend, erecv,
    in_sem, x_sem, s0_sem, t0_sem, s1_sem, t1_sem, s2_sem, t2_sem, s3_sem, t3_sem, se_sem, te_sem,
):
    num_vars = w_ref.shape[0]
    width = w_ref.shape[1]
    num_freq, modes_kept = vec_ref.shape[0], vec_ref.shape[2]
    total_rows = num_freq * 2 * modes_kept
    rows = total_rows // 4
    half = rows // 2
    inner = xbuf.shape[1] * xbuf.shape[2]
    space, blk = lax.axis_index("space"), lax.axis_index("blk")
    z, x = space // 2, space % 2
    y, c = blk // 2, blk % 2
    size = 2 * depth
    across_core = (space, y * 2 + (1 - c))
    across_x = (z * 2 + (1 - x), blk)
    across_y = (space, (1 - y) * 2 + c)

    small = []
    for k, (src, dst) in enumerate(
        ((freq_hbm, freq_ref), (off_hbm, off_ref), (vec_hbm, vec_ref), (w_hbm, w_ref))
    ):
        copy = pltpu.make_async_copy(src, dst, in_sem.at[k])
        copy.start()
        small.append(copy)
    chunks = [(d, v) for d in list(range(1, depth)) + [0] for v in range(num_vars)]
    loads = []
    for q, (d, v) in enumerate(chunks):
        cols = pl.ds(pl.multiple_of(lax.rem(z + d, depth) * (2 * width), 2 * width), 2 * width)
        load = pltpu.make_async_copy(x_ref.at[:, v, :, cols], xbuf.at[q], x_sem.at[q])
        load.start()
        loads.append(load)

    barrier = pltpu.get_barrier_semaphore()
    pl.semaphore_signal(barrier, inc=1, device_id=across_core, device_id_type=MESH)
    pl.semaphore_signal(barrier, inc=1, device_id=across_y, device_id_type=MESH)
    for d in range(1, size):
        pl.semaphore_signal(
            barrier, inc=1, device_id=(lax.rem(space + d, size), blk), device_id_type=MESH
        )

    for copy in small:
        copy.wait()
    matrix = projection_rows(
        freq_ref, off_ref, vec_ref[...], xbuf.shape[2], 2 * depth, space, blk
    )
    high = matrix.astype(jnp.bfloat16)
    low = (matrix - high.astype(jnp.float32)).astype(jnp.bfloat16)
    for ya in range(2):
        for ca in range(2):
            first = (ya * 2 + ca) * rows
            acat[0, (ca + c) % 2, (ya + y) % 2] = high[first : first + rows]
            acat[1, (ca + c) % 2, (ya + y) % 2] = low[first : first + rows]

    def project(q):
        for xa in range(2):
            xr = (x + xa) % 2
            block = xbuf[q, :, :, xa * width : (xa + 1) * width].reshape(inner, width)
            high = block.astype(jnp.bfloat16)
            low = (block - high.astype(jnp.float32)).astype(jnp.bfloat16)
            both = jnp.dot(
                acat[...].reshape(2 * total_rows, inner), high, preferred_element_type=jnp.float32
            )
            rest = jnp.dot(
                acat[0].reshape(total_rows, inner), low, preferred_element_type=jnp.float32
            )
            res = both[:total_rows] + (both[total_rows:] + rest)
            for cr, buf in ((0, keep), (1, send0)):
                for yr in range(2):
                    first = (cr * 2 + yr) * rows
                    buf[q, 0, xr, yr] = res[first : first + half]
                    buf[q, 1, yr, xr] = res[first + half : first + rows]

    def remote(src, dst, sem_out, sem_in, target):
        return pltpu.make_async_remote_copy(
            src_ref=src, dst_ref=dst, send_sem=sem_out, recv_sem=sem_in,
            device_id=target, device_id_type=MESH,
        )

    count = len(chunks)
    hop0 = [
        remote(send0.at[q], r0.at[q], s0_sem.at[q], t0_sem.at[q], across_core)
        for q in range(count)
    ]
    hop1 = [
        [
            remote(keep.at[q, h, 1], r1.at[q, h], s1_sem.at[q, h], t1_sem.at[q, h], to)
            for h, to in ((0, across_x), (1, across_y))
        ]
        for q in range(count)
    ]
    hop2 = [
        [
            remote(r1.at[q, h, 1], r2.at[q, h], s2_sem.at[q, h], t2_sem.at[q, h], to)
            for h, to in ((0, across_y), (1, across_x))
        ]
        for q in range(count)
    ]
    hop3 = {}
    for q, (d, v) in enumerate(chunks):
        if d:
            hop3[d, v] = remote(
                s2.at[q], r3.at[v, d - 1], s3_sem.at[v, d - 1], t3_sem.at[v, d - 1],
                (lax.rem(z + d, depth) * 2 + x, blk),
            )

    def stage0(q):
        loads[q].wait()
        project(q)
        if q == 0:
            pl.semaphore_wait(barrier, size + 1)
        hop0[q].start()

    def stage1(q):
        hop0[q].wait_recv()
        for h in range(2):
            keep[q, h, 1] = keep[q, h, 1] + r0[q, h, 1]
            hop1[q][h].start()

    def stage2(q):
        for h in range(2):
            hop1[q][h].wait_recv()
            r1[q, h, 1] = r1[q, h, 1] + (keep[q, h, 0, 1] + r0[q, h, 0, 1])
            hop2[q][h].start()

    def stage3(q):
        for h in range(2):
            hop2[q][h].wait_recv()
            s2[q, h] = (keep[q, h, 0, 0] + r0[q, h, 0, 0]) + (r1[q, h, 0] + r2[q, h])
        d, v = chunks[q]
        if d:
            hop3[d, v].start()
            return
        result = s2[q]
        for d in range(1, depth):
            hop3[d, v].wait_recv()
            result = result + r3[v, d - 1]
        result = result.reshape(rows, width)
        raw[v] = result
        term = result * result * w_ref[v : v + 1, :]
        if v == 0:
            acc[...] = term
        else:
            acc[...] = acc[...] + term

    lags = (0, 2, 5, 8)
    for step in range(count + lags[-1]):
        for lag, stage in zip(lags, (stage0, stage1, stage2, stage3)):
            if 0 <= step - lag < count:
                stage(step - lag)

    def fold(value):
        folded = value[:, :LANES]
        for k in range(1, width // LANES):
            folded = folded + value[:, k * LANES : (k + 1) * LANES]
        return folded

    diagonal = lax.broadcasted_iota(jnp.int32, (rows, LANES), 0) == lax.broadcasted_iota(
        jnp.int32, (rows, LANES), 1
    )
    last = lax.broadcasted_iota(jnp.int32, (1, LANES), 1) == rows
    row_sum = jnp.sum(fold(acc[...]), axis=1, keepdims=True)
    weight_sum = fold(jnp.sum(w_ref[...], axis=0, keepdims=True))
    weight_sum = jnp.sum(weight_sum, axis=1, keepdims=True)
    lane_sum = jnp.sum(jnp.where(diagonal, row_sum, 0.0), axis=0, keepdims=True)
    esend[...] = jnp.where(last, weight_sum, lane_sum)
    share = []
    for d in range(1, size):
        copy = remote(
            esend, erecv.at[d - 1], se_sem.at[d - 1], te_sem.at[d - 1],
            (lax.rem(space + d, size), blk),
        )
        copy.start()
        share.append(copy)
    total = esend[...]
    for d in range(1, size):
        share[d - 1].wait_recv()
        total = total + erecv[d - 1]
    owned = rows // (2 * modes_kept)
    weight_total = jnp.sum(jnp.where(last, total, 0.0), axis=1, keepdims=True)
    pair = jnp.sum(jnp.where(diagonal, total, 0.0), axis=1, keepdims=True)
    pair = pair.reshape(owned, 2 * modes_kept, 1)
    pair = pair + jnp.concatenate([pair[:, modes_kept:], pair[:, :modes_kept]], axis=1)
    energy = pair / (num_blocks * weight_total)[None]
    inverse = 1.0 / jnp.sqrt(num_blocks * energy + 1e-06)
    for v in range(num_vars):
        scaled = raw[v].reshape(owned, 2 * modes_kept, width) * inverse
        out_ref[:, 0, v] = scaled[:, :modes_kept]
        out_ref[:, 1, v] = scaled[:, modes_kept:]
    square = (modes_kept, modes_kept)
    same = lax.broadcasted_iota(jnp.int32, square, 0) == lax.broadcasted_iota(jnp.int32, square, 1)
    spread = jnp.broadcast_to(energy[:, :modes_kept], (owned, modes_kept, modes_kept))
    energy_ref[...] = jnp.sum(jnp.where(same[None], spread, 0.0), axis=1)
    for q in range(count):
        hop0[q].wait_send()
        for copy in hop1[q] + hop2[q]:
            copy.wait_send()
    for copy in list(hop3.values()) + share:
        copy.wait_send()


def reduce_modes(snapshots, weights, vectors, frequencies, offsets):
    items, num_vars, times, cells = snapshots.shape
    num_freq, _, modes_kept, num_blocks = vectors.shape
    width = weights.shape[1]
    depth = cells // width // 2
    owned = num_freq // 4
    rows = owned * 2 * modes_kept
    inner = items * times
    half = rows // 2
    size = 2 * depth
    chunks = depth * num_vars
    f32 = jnp.float32
    dma = pltpu.SemaphoreType.DMA
    anywhere = pl.BlockSpec(memory_space=pl.ANY)
    vmem = pl.BlockSpec(memory_space=pltpu.VMEM)
    return pl.pallas_call(
        functools.partial(reduce_kernel, depth, num_blocks),
        out_shape=(
            jax.ShapeDtypeStruct((owned, 2, num_vars, modes_kept, width), f32),
            jax.ShapeDtypeStruct((owned, modes_kept), f32),
        ),
        in_specs=[anywhere] * 5,
        out_specs=(vmem, vmem),
        scratch_shapes=[
            pltpu.VMEM((chunks, items, times, 2 * width), f32),
            pltpu.VMEM((num_vars, width), f32),
            pltpu.VMEM(vectors.shape, f32),
            pltpu.SMEM(frequencies.shape, jnp.int32),
            pltpu.SMEM(offsets.shape, jnp.int32),
            pltpu.VMEM((num_vars, rows, width), f32),
            pltpu.VMEM((2, 2, 2, rows, inner), jnp.bfloat16),
            pltpu.VMEM((chunks, 2, 2, 2, half, width), f32),
            pltpu.VMEM((chunks, 2, 2, 2, half, width), f32),
            pltpu.VMEM((chunks, 2, 2, 2, half, width), f32),
            pltpu.VMEM((chunks, 2, 2, half, width), f32),
            pltpu.VMEM((chunks, 2, half, width), f32),
            pltpu.VMEM((chunks, 2, half, width), f32),
            pltpu.VMEM((num_vars, depth - 1, 2, half, width), f32),
            pltpu.VMEM((rows, width), f32),
            pltpu.VMEM((1, LANES), f32),
            pltpu.VMEM((size - 1, 1, LANES), f32),
            dma((4,)),
            dma((chunks,)),
            dma((chunks,)),
            dma((chunks,)),
            dma((chunks, 2)),
            dma((chunks, 2)),
            dma((chunks, 2)),
            dma((chunks, 2)),
            dma((num_vars, depth - 1)),
            dma((num_vars, depth - 1)),
            dma((size - 1,)),
            dma((size - 1,)),
        ],
        compiler_params=pltpu.CompilerParams(
            collective_id=0, has_side_effects=True, vmem_limit_bytes=56 * 2**20
        ),
    )(snapshots, weights, vectors, frequencies, offsets)


def local_kernel(snapshots, weights, frequencies, offsets, eigenvectors):
    modes, energies = reduce_modes(
        snapshots.transpose(0, 2, 1, 3), weights, eigenvectors.transpose(0, 1, 3, 2),
        frequencies, offsets,
    )
    return (modes.transpose(0, 1, 3, 2, 4), energies)


def fits(mesh):
    return mesh.shape["blk"] == 4 and mesh.shape["space"] == 8


def solution(mesh):
    local = local_kernel if fits(mesh) else local_plain
    in_specs = (P("blk", "space", None, None), P(None, "space"), P(), P("blk"), P())
    out_specs = (P("blk", None, None, None, "space"), P("blk", None))
    return jax.shard_map(local, mesh=mesh, in_specs=in_specs, out_specs=out_specs, check_vma=False)
```
